512 devices in a mesh: row: 16 (over y, z_hi, core), col: 32 (over x, z_lo).
Axes of the slice: x: 4, y: 4, z: 16 (z_hi: 2, z_lo: 8; z = z_hi * 8 + z_lo), core: 2. Of those that a mesh axis runs over, the one named last changes fastest.
Arguments:
- amplitudes: bfloat16 [96, 16384], P(None, ('row', 'col')), may hold values from -6 to 6
- integrals: bfloat16 [16384, 16384], P('row', 'col'), may hold values from -0.046875 to 0.046875
- owner: int32 [128, 128], replicated, may hold values from 0 to 1, as said below
Outputs:
- residual: float32 [96, 16384], P(None, ('row', 'col'))
The draws below stay inside these ranges and needn't reach their ends.
Inputs may be any that keep to these rules, and one draw needn't show every extreme that they name: owner[I, J] + owner[J, I] = 1 for I != J, and owner[I, I] = 1.
All inputs are finite; a program needn't handle non-finite values.
Results may differ from the reference program's by a relative error of at most 0.0003.
Values may be sent and summed in bfloat16 or wider, within the bound.
A program may use at most 64 MiB of HBM per device.

```python
import jax
import jax.numpy as jnp
from jax import lax

TB = 128
OCC = 96
NBLK = 128
PAIRS = 16384


def draw_owner(key, part):
    key = jax.random.fold_in(key, 11)
    random_bits = jax.random.randint(key, (NBLK, NBLK), 0, 2, dtype=jnp.int32)
    row_ids = jnp.arange(NBLK, dtype=jnp.int32)[:, None]
    col_ids = jnp.arange(NBLK, dtype=jnp.int32)[None, :]
    lower_part = jnp.where(row_ids > col_ids, 1 - random_bits.T, jnp.ones_like(random_bits))
    return jnp.where(row_ids < col_ids, random_bits, lower_part).astype(jnp.int32)


def block_scale(rng, dims, split, least, high):
    factor_of, own = 1.0, jax.random.fold_in(rng, 6)
    for dim, parts in split:
        heights = jnp.exp(jax.random.uniform(jax.random.fold_in(own, dim), (parts,), jnp.float32, least / len(split), high / len(split)))
        factor_of = factor_of * jnp.repeat(heights, dims[dim] // parts).reshape([-1 if axis == dim else 1 for axis in range(len(dims))])
    return factor_of


def normal_values(key, extent, scale, limit, split=(), kind=jnp.bfloat16):
    result = scale * jax.random.normal(key, extent, jnp.float32)
    if split:
        result = result * block_scale(key, extent, split, -0.22, 0.18)
    return jnp.clip(result, -limit, limit).astype(kind)


def setup_inputs(seed: int = 0) -> dict:
    arg_keys = jax.random.split(jax.random.key(seed), 4)
    amplitudes = normal_values(arg_keys[0], (OCC, PAIRS), 1.0, 6.0, ((1, 512),))
    integrals = normal_values(arg_keys[1], (PAIRS, PAIRS), PAIRS ** -0.5, 0.046875, ((0, 16), (1, 32)))
    owner = draw_owner(jax.random.fold_in(arg_keys[3], 71), 0)
    return {"amplitudes": amplitudes, "integrals": integrals, "owner": owner}


def reference(amplitudes, integrals, owner):
    blocks = owner.shape[0]
    amp_rows = amplitudes.shape[0]
    block_ids = jnp.arange(blocks, dtype=jnp.int32)

    def accumulate(column_sum, block_index):
        row_slab = lax.dynamic_slice_in_dim(integrals, block_index * TB, TB, 0)
        held_row = lax.dynamic_slice_in_dim(owner, block_index, 1, 0)[0]
        slab_grid = row_slab.reshape(TB, blocks, TB)
        zero_grid = jnp.zeros_like(slab_grid)
        kept_tiles = jnp.where((held_row == 1)[None, :, None], slab_grid, zero_grid).reshape(TB, blocks * TB)
        away_held = (held_row == 1) & (block_ids != block_index)
        away_tiles = jnp.where(away_held[None, :, None], slab_grid, zero_grid).reshape(TB, blocks * TB)
        rows_term = lax.dot_general(amplitudes, kept_tiles, (((1,), (1,)), ((), ())), preferred_element_type=jnp.float32)
        local_amps = lax.dynamic_slice_in_dim(amplitudes, block_index * TB, TB, 1)
        column_sum = column_sum + jnp.dot(local_amps, away_tiles, preferred_element_type=jnp.float32)
        return column_sum, rows_term

    start_sum = jnp.zeros((amp_rows, blocks * TB), jnp.float32)
    column_sum, row_terms = lax.scan(accumulate, start_sum, block_ids)
    row_whole = jnp.transpose(row_terms, (1, 0, 2)).reshape(amp_rows, blocks * TB)
    return row_whole + column_sum
```

```python
import functools

import jax
import jax.numpy as jnp
from jax import lax
from jax.experimental import pallas as pl
from jax.experimental.pallas import tpu as pltpu
from jax.sharding import PartitionSpec as P

TB = 128
LANES = 128
XN, ZN = 4, 8
MESH = pl.DeviceIdType.MESH
F32 = jnp.float32
BF16 = jnp.bfloat16


def pack(block, occ):
    lane = lax.broadcasted_iota(jnp.int32, (8, LANES), 1)
    out = []
    for s in range(block.shape[0] // 32):
        last = block[s * 32 + 24 : s * 32 + 32]
        for j in range(3):
            moved = pltpu.roll(last, occ - 32 * j, 1)
            out.append(jnp.where(lane < occ, block[s * 32 + 8 * j : s * 32 + 8 * j + 8], moved))
    return jnp.concatenate(out, axis=0)


def unpack(block, occ):
    lane = lax.broadcasted_iota(jnp.int32, (8, LANES), 1)
    last = jnp.zeros((8, LANES), F32)
    for j in range(3):
        moved = pltpu.roll(block[8 * j : 8 * j + 8], (LANES - occ + 32 * j) % LANES, 1)
        last = jnp.where((lane >= 32 * j) & (lane < 32 * j + 32), moved, last)
    return jnp.concatenate([block, last], axis=0)


def kernel(
    amp_ref, w_hbm, owner_hbm, out_ref,
    w_v, wat, own_s, ar, ac, row_send, x_recv, col_half, sib_recv, cross_send, cross_recv, z_send, z_recv,
    w_sem, own_sem, sems_a, sems_b, sems_c, sems_d, sems_e,
):
    occ, shard = amp_ref.shape
    rows, cols = w_v.shape
    row_tiles, col_tiles = rows // TB, cols // TB
    chunk = rows // XN
    packed = chunk * 3 // 4
    piece = packed // ZN
    r = lax.axis_index("row")
    c = lax.axis_index("col")
    y, zh, core = r // 4, (r // 2) % 2, r % 2
    x, zl = c // 8, c % 8

    def at(yy, zz, cc, xx, ll):
        return (yy * 4 + zz * 2 + cc, xx * 8 + ll)

    z_peers = [at(y, zh, core, x, zl ^ k) for k in range(1, ZN)]
    x_peers = [at(y, zh, core, x ^ k, zl) for k in range(1, XN)]
    sibling = at(y, zh, 1 - core, x, zl)
    target = at((zl % 4) ^ 1, zl // 4, x % 2, y, 4 * zh + 2 * core + x // 2)
    source = at(x, zl // 4, (zl // 2) % 2, 2 * (zl % 2) + core, 4 * zh + (y ^ 1))

    w_copy = pltpu.make_async_copy(w_hbm, w_v, w_sem)
    w_copy.start()
    own_copy = pltpu.make_async_copy(owner_hbm.at[pl.ds(r * row_tiles, row_tiles)], own_s, own_sem)
    own_copy.start()

    eye = (
        lax.broadcasted_iota(jnp.int32, (shard, shard), 0) == lax.broadcasted_iota(jnp.int32, (shard, shard), 1)
    ).astype(F32).astype(BF16)
    wide = jnp.concatenate([amp_ref[...], jnp.zeros((LANES - occ, shard), BF16)], axis=0)
    turned = lax.dot_general(eye, wide, (((1,), (1,)), ((), ())), preferred_element_type=F32)
    mine = pl.ds(pl.multiple_of(x * chunk + zl * shard, shard), shard)
    ar[mine, :] = turned.astype(BF16)

    barrier = pltpu.get_barrier_semaphore()
    partners = z_peers + x_peers + [sibling, target, source]
    for peer in partners:
        pl.semaphore_signal(barrier, inc=1, device_id=peer, device_id_type=MESH)
    pl.semaphore_wait(barrier, len(partners))

    def send(src, dst, sems, k, peer):
        copy = pltpu.make_async_remote_copy(
            src_ref=src, dst_ref=dst, send_sem=sems.at[0, k], recv_sem=sems.at[1, k],
            device_id=peer, device_id_type=MESH,
        )
        copy.start()
        return copy

    za = [send(ar.at[mine], ar.at[mine], sems_a, k, z_peers[k]) for k in reversed(range(ZN - 1))]

    w_copy.wait()
    own_copy.wait()
    for i in range(row_tiles):
        for j in range(col_tiles):
            held = own_s[i, c * col_tiles + j] == 1
            tile = w_v[i * TB : (i + 1) * TB, j * TB : (j + 1) * TB]
            kept = jnp.where(held, tile, jnp.zeros_like(tile))
            w_v[i * TB : (i + 1) * TB, j * TB : (j + 1) * TB] = kept
            away = jnp.where(r * row_tiles + i == c * col_tiles + j, jnp.zeros_like(tile), kept)
            wat[j * TB : (j + 1) * TB, i * TB : (i + 1) * TB] = away.T
    for copy in za:
        copy.wait()

    own_chunk = pl.ds(pl.multiple_of(x * chunk, chunk), chunk)
    cross_in = send(
        ar.at[own_chunk], ac.at[pl.ds(pl.multiple_of((x % 2) * chunk, chunk), chunk)], sems_c, 0, target
    )
    xa = [send(ar.at[own_chunk], ar.at[own_chunk], sems_b, k, x_peers[k]) for k in (1, 0, 2)]

    cross_in.wait()
    half = pl.ds(pl.multiple_of(core * chunk, chunk), chunk)
    other = pl.ds(pl.multiple_of((1 - core) * chunk, chunk), chunk)
    sib_in = send(ac.at[half], ac.at[half], sems_c, 1, sibling)
    for copy in xa:
        copy.wait()

    col_half[0] = pack(jnp.dot(wat[other, :], ar[...], preferred_element_type=F32), occ)
    sib_out = send(col_half.at[0], sib_recv, sems_c, 2, sibling)
    sib_in.wait()

    xd = []
    for k in (1, 0, 2):
        theirs = pl.ds(pl.multiple_of((x ^ (k + 1)) * chunk, chunk), chunk)
        row_send[k] = pack(jnp.dot(w_v[theirs, :], ac[...], preferred_element_type=F32), occ)
        xd.append(send(row_send.at[k], x_recv.at[k], sems_d, k, x_peers[k]))
    own_cols = pack(jnp.dot(wat[half, :], ar[...], preferred_element_type=F32), occ)
    sib_out.wait()
    cross_send[...] = own_cols + sib_recv[...]
    cross_out = send(cross_send, cross_recv, sems_c, 3, source)
    own_rows = pack(jnp.dot(w_v[own_chunk, :], ac[...], preferred_element_type=F32), occ)
    for copy in xd:
        copy.wait()
    total = own_rows + x_recv[0] + x_recv[1] + x_recv[2]
    cross_out.wait()
    z_send[...] = total + cross_recv[...]

    ze = []
    for k in reversed(range(ZN - 1)):
        part = pl.ds(pl.multiple_of((zl ^ (k + 1)) * piece, piece), piece)
        ze.append(send(z_send.at[part], z_recv.at[k], sems_e, k, z_peers[k]))
    result = z_send[pl.ds(pl.multiple_of(zl * piece, piece), piece), :]
    for copy in ze:
        copy.wait()
    for k in range(ZN - 1):
        result = result + z_recv[k]
    out_ref[...] = unpack(result, occ)


def local(amplitudes, integrals, owner):
    occ, shard = amplitudes.shape
    rows, cols = integrals.shape
    chunk = rows // XN
    packed = chunk * 3 // 4
    dma = pltpu.SemaphoreType.DMA
    turned = pl.pallas_call(
        kernel,
        out_shape=jax.ShapeDtypeStruct((shard, LANES), F32),
        in_specs=[
            pl.BlockSpec(memory_space=pltpu.VMEM),
            pl.BlockSpec(memory_space=pl.ANY),
            pl.BlockSpec(memory_space=pl.ANY),
        ],
        out_specs=pl.BlockSpec(memory_space=pltpu.VMEM),
        scratch_shapes=[
            pltpu.VMEM((rows, cols), BF16),
            pltpu.VMEM((cols, rows), BF16),
            pltpu.SMEM((rows // TB, owner.shape[1]), jnp.int32),
            pltpu.VMEM((rows, LANES), BF16),
            pltpu.VMEM((cols, LANES), BF16),
            pltpu.VMEM((XN - 1, packed, LANES), F32),
            pltpu.VMEM((XN - 1, packed, LANES), F32),
            pltpu.VMEM((1, packed, LANES), F32),
            pltpu.VMEM((packed, LANES), F32),
            pltpu.VMEM((packed, LANES), F32),
            pltpu.VMEM((packed, LANES), F32),
            pltpu.VMEM((packed, LANES), F32),
            pltpu.VMEM((ZN - 1, packed // ZN, LANES), F32),
            dma,
            dma,
            dma((2, ZN - 1)),
            dma((2, XN - 1)),
            dma((2, 4)),
            dma((2, XN - 1)),
            dma((2, ZN - 1)),
        ],
        compiler_params=pltpu.CompilerParams(
            collective_id=0, has_side_effects=True, vmem_limit_bytes=24 * 1024 * 1024
        ),
    )(amplitudes, integrals, owner)
    return turned[:, :occ].T


def solution(mesh):
    in_specs = (P(None, ("row", "col")), P("row", "col"), P())
    out_specs = P(None, ("row", "col"))
    return jax.shard_map(local, mesh=mesh, in_specs=in_specs, out_specs=out_specs, check_vma=False)
```

```python
import jax
import jax.numpy as jnp
from jax import lax
from jax.experimental import pallas as pl
from jax.experimental.pallas import tpu as pltpu
from jax.sharding import PartitionSpec as P

TB = 128
LANES = 128
XN, YN, ZN, HN = 4, 4, 8, 2
MESH = pl.DeviceIdType.MESH
F32 = jnp.float32
BF16 = jnp.bfloat16


def pack(block, occ):
    lane = lax.broadcasted_iota(jnp.int32, (8, LANES), 1)
    out = []
    for s in range(block.shape[0] // 32):
        last = block[s * 32 + 24 : s * 32 + 32]
        for j in range(3):
            moved = pltpu.roll(last, occ - 32 * j, 1)
            out.append(jnp.where(lane < occ, block[s * 32 + 8 * j : s * 32 + 8 * j + 8], moved))
    return jnp.concatenate(out, axis=0)


def unpack(block, occ):
    lane = lax.broadcasted_iota(jnp.int32, (8, LANES), 1)
    last = jnp.zeros((8, LANES), F32)
    for j in range(3):
        moved = pltpu.roll(block[8 * j : 8 * j + 8], (LANES - occ + 32 * j) % LANES, 1)
        last = jnp.where((lane >= 32 * j) & (lane < 32 * j + 32), moved, last)
    return jnp.concatenate([block, last], axis=0)


def kernel(
    amp_hbm, w_hbm, owner_hbm, out_ref,
    amp_v, w_v, wat, own_s, ar, ac, row_send, x_recv, col_half, sib_recv, col_send, col_recv, z_send, z_recv,
    copy_sems, za_sems, xa_sems, ci_sems, sib_sems, co_sems, xd_sems, ze_sems,
):
    shard, occ = amp_v.shape
    rows, cols = w_v.shape
    row_tiles, col_tiles = rows // TB, cols // TB
    chunk = rows // XN
    packed = chunk * 3 // 4
    piece = packed // ZN
    r = lax.axis_index("row")
    c = lax.axis_index("col")
    y, zh, core = r // 4, (r // 2) % 2, r % 2
    x, zl = c // 8, c % 8

    def at(yy, zz, cc, xx, ll):
        return (yy * 4 + zz * 2 + cc, xx * 8 + ll)

    def rows_at(start, size, unit=8):
        return pl.ds(pl.multiple_of(start, unit), size)

    z_peers = [at(y, zh, core, x, zl ^ k) for k in range(1, ZN)]
    x_peers = [at(y, zh, core, x ^ k, zl) for k in range(1, XN)]
    sibling = at(y, zh, 1 - core, x, zl)
    spots = [(yy, hh) for hh in range(HN) for yy in range(YN)]
    reader_line = 4 * zh + 2 * core + x // 2
    readers = [at(yy, hh, x % 2, y, reader_line) for yy, hh in spots]
    writers = [at(x, zl // 4, (zl // 2) % 2, 2 * (zl % 2) + core, l) for l in range(ZN)]
    fixed = (x == y) & (core == x % 2) & (zl == reader_line)
    reads_self = [fixed & (y == yy) & (zh == hh) for yy, hh in spots]
    writes_self = [fixed & (zl == l) for l in range(ZN)]

    amp_copy = pltpu.make_async_copy(amp_hbm, amp_v, copy_sems.at[0])
    amp_copy.start()
    own_copy = pltpu.make_async_copy(owner_hbm.at[rows_at(r * row_tiles, row_tiles)], own_s, copy_sems.at[1])
    own_copy.start()
    w_copy = pltpu.make_async_copy(w_hbm, w_v, copy_sems.at[2])
    w_copy.start()

    barrier = pltpu.get_barrier_semaphore()

    def hello(peer):
        pl.semaphore_signal(barrier, inc=1, device_id=peer, device_id_type=MESH)

    for peer in z_peers + x_peers + [sibling]:
        hello(peer)
    for peer, own in zip(readers + writers, reads_self + writes_self):
        pl.when(jnp.logical_not(own))(lambda peer=peer: hello(peer))

    amp_copy.wait()
    mine = rows_at(x * chunk + zl * shard, shard, 32)
    ar[mine, :] = jnp.concatenate([amp_v[...], jnp.zeros((shard, LANES - occ), BF16)], axis=1)
    greeted = ZN - 1 + XN - 1 + 1 + len(readers) + len(writers)
    pl.semaphore_wait(barrier, greeted - 2 * fixed.astype(jnp.int32))

    def remote(src, dst, send_sem, recv_sem, peer):
        return pltpu.make_async_remote_copy(
            src_ref=src, dst_ref=dst, send_sem=send_sem, recv_sem=recv_sem, device_id=peer, device_id_type=MESH
        )

    def start(*args):
        copy = remote(*args)
        copy.start()
        return copy

    sent = []

    za = [None] * (ZN - 1)
    for k in reversed(range(ZN - 1)):
        za[k] = start(ar.at[mine], ar.at[mine], za_sems.at[0, k], za_sems.at[1, k], z_peers[k])
    sent += za
    ci_slot = rows_at((x % 2) * chunk + zl * shard, shard, 32)
    ci = []
    for k in range(len(spots)):
        copy = remote(ar.at[mine], ac.at[ci_slot], ci_sems.at[0, k], ci_sems.at[1, zl], readers[k])
        pl.when(jnp.logical_not(reads_self[k]))(copy.start)
        ci.append(copy)

    @pl.when(fixed)
    def _():
        pltpu.make_async_copy(ar.at[mine], ac.at[ci_slot], ci_sems.at[1, zl]).start()

    w_copy.wait()
    own_copy.wait()
    for i in range(row_tiles):
        for j in range(col_tiles):
            held = own_s[i, c * col_tiles + j] == 1
            tile = w_v[i * TB : (i + 1) * TB, j * TB : (j + 1) * TB]
            kept = jnp.where(held, tile, jnp.zeros_like(tile))
            w_v[i * TB : (i + 1) * TB, j * TB : (j + 1) * TB] = kept
            away = jnp.where(r * row_tiles + i == c * col_tiles + j, jnp.zeros_like(tile), kept)
            wat[j * TB : (j + 1) * TB, i * TB : (i + 1) * TB] = away.T

    groups = [(zl // 4 * 4, 4, (0, 1, 2)), ((zl ^ 4) // 2 * 2, 2, (3, 4)), ((zl ^ 6) // 2 * 2, 2, (5, 6))]
    xa = []
    for g, (first, count, waits) in enumerate(groups):
        for k in waits:
            za[k].wait_recv()
        part = rows_at(x * chunk + first * shard, count * shard, 32)
        for k in (1, 0, 2):
            xa.append(start(ar.at[part], ar.at[part], xa_sems.at[0, g, k], xa_sems.at[1, g, k], x_peers[k]))
    sent += xa

    half = rows_at(core * chunk, chunk, 256)
    other = rows_at((1 - core) * chunk, chunk, 256)
    for copy in xa:
        copy.wait_recv()

    col_half[...] = pack(jnp.dot(wat[other, :], ar[...], preferred_element_type=F32), occ)
    sib_out = start(col_half, sib_recv, sib_sems.at[0, 1], sib_sems.at[1, 1], sibling)

    for l in range(ZN):
        slot = rows_at(core * chunk + l * shard, shard, 32)
        remote(ar.at[mine], ac.at[slot], ci_sems.at[0, 0], ci_sems.at[1, l], sibling).wait_recv()
    sib_in = start(ac.at[half], ac.at[half], sib_sems.at[0, 0], sib_sems.at[1, 0], sibling)
    own_cols = pack(jnp.dot(wat[half, :], ar[...], preferred_element_type=F32), occ)
    sib_out.wait_recv()
    col_send[...] = own_cols + sib_recv[...]
    co = []
    for l in range(ZN):
        part = pl.ds(l * piece, piece)
        copy = remote(col_send.at[part], col_recv.at[zh * YN + y], co_sems.at[0, l], co_sems.at[1, zh * YN + y], writers[l])
        pl.when(jnp.logical_not(writes_self[l]))(copy.start)
        co.append(copy)

    @pl.when(fixed)
    def _():
        pltpu.make_async_copy(
            col_send.at[rows_at(zl * piece, piece)], col_recv.at[zh * YN + y], co_sems.at[1, zh * YN + y]
        ).start()

    sib_in.wait_recv()
    outs = list(reversed(groups))
    xd = [[None] * (XN - 1) for _ in outs]

    def leave(g, k):
        first, count, _ = outs[g]
        part = rows_at(first * piece, count * piece)
        xd[g][k] = start(
            row_send.at[k, part], x_recv.at[k, part], xd_sems.at[0, g, k], xd_sems.at[1, g, k], x_peers[k]
        )

    for k in (1, 0, 2):
        theirs = rows_at((x ^ (k + 1)) * chunk, chunk, 256)
        row_send[k] = pack(jnp.dot(w_v[theirs, :], ac[...], preferred_element_type=F32), occ)
        leave(0, k)
    for g in range(1, len(outs)):
        for k in (1, 0, 2):
            leave(g, k)
    z_send[...] = pack(jnp.dot(w_v[rows_at(x * chunk, chunk, 256), :], ac[...], preferred_element_type=F32), occ)

    ze = []
    for g, (first, count, waits) in enumerate(outs):
        for copy in xd[g]:
            copy.wait_recv()
        part = rows_at(first * piece, count * piece)
        total = z_send[part, :]
        for k in range(XN - 1):
            total = total + x_recv[k, part, :]
        z_send[part, :] = total
        for k in reversed(waits):
            where = rows_at((zl ^ (k + 1)) * piece, piece)
            ze.append(start(z_send.at[where], z_recv.at[k], ze_sems.at[0, k], ze_sems.at[1, k], z_peers[k]))
    sent += [copy for line in xd for copy in line] + ze + [sib_in, sib_out]

    result = z_send[rows_at(zl * piece, piece), :]
    for copy in ze:
        copy.wait_recv()
    for k in range(ZN - 1):
        result = result + z_recv[k]
    for k in range(len(spots)):
        part = pl.ds(0, piece)
        remote(col_send.at[part], col_recv.at[k], co_sems.at[0, 0], co_sems.at[1, k], sibling).wait_recv()
    for k in range(len(spots)):
        result = result + col_recv[k]
    out_ref[...] = unpack(result, occ)[:, :occ]

    for copy in sent:
        copy.wait_send()
    for copies, own in ((ci, reads_self), (co, writes_self)):
        for copy, to_self in zip(copies, own):
            pl.when(jnp.logical_not(to_self))(copy.wait_send)


def local(amplitudes, integrals, owner):
    occ, shard = amplitudes.shape
    rows, cols = integrals.shape
    packed = rows // XN * 3 // 4
    piece = packed // ZN
    dma = pltpu.SemaphoreType.DMA
    hbm = pl.BlockSpec(memory_space=pltpu.HBM)
    turned = pl.pallas_call(
        kernel,
        out_shape=jax.ShapeDtypeStruct((shard, occ), F32),
        in_specs=[hbm, hbm, hbm],
        out_specs=pl.BlockSpec(memory_space=pltpu.VMEM),
        scratch_shapes=[
            pltpu.VMEM((shard, occ), BF16),
            pltpu.VMEM((rows, cols), BF16),
            pltpu.VMEM((cols, rows), BF16),
            pltpu.SMEM((rows // TB, owner.shape[1]), jnp.int32),
            pltpu.VMEM((rows, LANES), BF16),
            pltpu.VMEM((cols, LANES), BF16),
            pltpu.VMEM((XN - 1, packed, LANES), F32),
            pltpu.VMEM((XN - 1, packed, LANES), F32),
            pltpu.VMEM((packed, LANES), F32),
            pltpu.VMEM((packed, LANES), F32),
            pltpu.VMEM((packed, LANES), F32),
            pltpu.VMEM((YN * HN, piece, LANES), F32),
            pltpu.VMEM((packed, LANES), F32),
            pltpu.VMEM((ZN - 1, piece, LANES), F32),
            dma((3,)),
            dma((2, ZN - 1)),
            dma((2, 3, XN - 1)),
            dma((2, ZN)),
            dma((2, 2)),
            dma((2, ZN)),
            dma((2, 3, XN - 1)),
            dma((2, ZN - 1)),
        ],
        compiler_params=pltpu.CompilerParams(
            collective_id=0, has_side_effects=True, vmem_limit_bytes=16 * 1024 * 1024
        ),
    )(amplitudes.T, integrals, owner)
    return turned.T


def solution(mesh):
    in_specs = (P(None, ("row", "col")), P("row", "col"), P())
    out_specs = P(None, ("row", "col"))
    return jax.shard_map(local, mesh=mesh, in_specs=in_specs, out_specs=out_specs, check_vma=False)
```

```python
import jax
import jax.numpy as jnp
from jax import lax
from jax.experimental import pallas as pl
from jax.experimental.pallas import tpu as pltpu
from jax.sharding import PartitionSpec as P

TB = 128
LANES = 128
XN, YN, ZN, HN = 4, 4, 8, 2
MESH = pl.DeviceIdType.MESH
F32 = jnp.float32
BF16 = jnp.bfloat16


def pack(block, occ):
    lane = lax.broadcasted_iota(jnp.int32, (8, LANES), 1)
    out = []
    for s in range(block.shape[0] // 32):
        last = block[s * 32 + 24 : s * 32 + 32]
        for j in range(3):
            moved = pltpu.roll(last, occ - 32 * j, 1)
            out.append(jnp.where(lane < occ, block[s * 32 + 8 * j : s * 32 + 8 * j + 8], moved))
    return jnp.concatenate(out, axis=0)


def unpack(block, occ):
    lane = lax.broadcasted_iota(jnp.int32, (8, LANES), 1)
    last = jnp.zeros((8, LANES), F32)
    for j in range(3):
        moved = pltpu.roll(block[8 * j : 8 * j + 8], (LANES - occ + 32 * j) % LANES, 1)
        last = jnp.where((lane >= 32 * j) & (lane < 32 * j + 32), moved, last)
    return jnp.concatenate([block, last], axis=0)


def kernel(
    amp_hbm, w_hbm, owner_hbm, out_ref,
    amp_v, w_v, wat, own_s, ar, ac, row_send, x_recv, col_all, team_recv, col_send, col_recv, z_send, z_recv,
    copy_sems, za_sems, xa_sems, ci_sems, ga_sems, gd_sems, co_sems, xd_sems, ze_sems,
):
    shard, occ = amp_v.shape
    rows, cols = w_v.shape
    row_tiles, col_tiles = rows // TB, cols // TB
    chunk = rows // XN
    packed = chunk * 3 // 4
    piece = packed // ZN
    r = lax.axis_index("row")
    c = lax.axis_index("col")
    y, zh, core = r // 4, (r // 2) % 2, r % 2
    x, zl = c // 8, c % 8

    def at(yy, zz, cc, xx, ll):
        return (yy * 4 + zz * 2 + cc, xx * 8 + ll)

    def rows_at(start, size, unit=8):
        return pl.ds(pl.multiple_of(start, unit), size)

    z_peers = [at(y, zh, core, x, zl ^ k) for k in range(1, ZN)]
    x_peers = [at(y, zh, core, x ^ k, zl) for k in range(1, XN)]
    mates = [(y ^ (m // 2), core ^ (m % 2)) for m in range(1, 2 * YN)]
    team = [at(yy, zh, cc, x, zl) for yy, cc in mates]
    pair = y ^ 1
    readers = [at((zl // 2) ^ 1, hh, x % 2, y, 4 * zh + 2 * core + x // 2) for hh in range(HN)]
    writers = [at(x, zl // 4, (zl // 2) % 2, 2 * (zl % 2) + core, 2 * pair + l) for l in range(2)]

    barrier = pltpu.get_barrier_semaphore()
    greeted = writers + z_peers[::-1] + team[::-1] + x_peers
    for peer in greeted:
        pl.semaphore_signal(barrier, inc=1, device_id=peer, device_id_type=MESH)

    amp_copy = pltpu.make_async_copy(amp_hbm, amp_v, copy_sems.at[0])
    amp_copy.start()
    own_copy = pltpu.make_async_copy(owner_hbm.at[rows_at(r * row_tiles, row_tiles)], own_s, copy_sems.at[1])
    own_copy.start()
    w_copy = pltpu.make_async_copy(w_hbm, w_v, copy_sems.at[2])
    w_copy.start()

    amp_copy.wait()
    mine = rows_at(x * chunk + zl * shard, shard, 32)
    ar[mine, :] = jnp.concatenate([amp_v[...], jnp.zeros((shard, LANES - occ), BF16)], axis=1)
    pl.semaphore_wait(barrier, len(greeted))

    def remote(src, dst, send_sem, recv_sem, peer):
        return pltpu.make_async_remote_copy(
            src_ref=src, dst_ref=dst, send_sem=send_sem, recv_sem=recv_sem, device_id=peer, device_id_type=MESH
        )

    sent = []

    def start(*args):
        copy = remote(*args)
        copy.start()
        sent.append(copy)
        return copy

    za = [None] * (ZN - 1)
    slot = rows_at((x % 2) * chunk + zl * shard, shard, 32)

    def to_line():
        for k in reversed(range(ZN - 1)):
            za[k] = start(ar.at[mine], ar.at[mine], za_sems.at[0, k], za_sems.at[1, k], z_peers[k])

    def to_readers():
        for k in range(HN):
            start(ar.at[mine], ac.at[slot], ci_sems.at[0, k], ci_sems.at[1, zl % 2], readers[k])

    to_readers()
    to_line()

    w_copy.wait()
    own_copy.wait()
    for i in range(row_tiles):
        for j in range(col_tiles):
            held = own_s[i, c * col_tiles + j] == 1
            tile = w_v[i * TB : (i + 1) * TB, j * TB : (j + 1) * TB]
            kept = jnp.where(held, tile, jnp.zeros_like(tile))
            w_v[i * TB : (i + 1) * TB, j * TB : (j + 1) * TB] = kept
            away = jnp.where(r * row_tiles + i == c * col_tiles + j, jnp.zeros_like(tile), kept)
            wat[j * TB : (j + 1) * TB, i * TB : (i + 1) * TB] = away.T

    groups = [(zl // 4 * 4, 4, (0, 1, 2)), ((zl ^ 4) // 2 * 2, 2, (3, 4)), ((zl ^ 6) // 2 * 2, 2, (5, 6))]
    xa = []
    for g, (first, count, waits) in enumerate(groups):
        for k in waits:
            za[k].wait_recv()
        part = rows_at(x * chunk + first * shard, count * shard, 32)
        for k in (1, 0, 2):
            xa.append(start(ar.at[part], ar.at[part], xa_sems.at[0, g, k], xa_sems.at[1, g, k], x_peers[k]))

    fetched = rows_at(core * chunk + pair * 2 * shard, 2 * shard, 64)

    def share():
        for l in range(2):
            remote(ar.at[mine], ac.at[slot], ci_sems.at[0, 0], ci_sems.at[1, l], writers[l]).wait_recv()
        return [
            start(ac.at[fetched], ac.at[fetched], ga_sems.at[0, m], ga_sems.at[1, m], team[m])
            for m in reversed(range(len(team)))
        ]

    outs = list(reversed(groups))
    xd = [[None] * (XN - 1) for _ in outs]

    def leave(g, k):
        first, count, _ = outs[g]
        part = rows_at(first * piece, count * piece)
        xd[g][k] = start(
            row_send.at[k, part], x_recv.at[k, part], xd_sems.at[0, g, k], xd_sems.at[1, g, k], x_peers[k]
        )

    def row_terms():
        for k in (1, 0, 2):
            theirs = rows_at((x ^ (k + 1)) * chunk, chunk, 256)
            row_send[k] = pack(jnp.dot(w_v[theirs, :], ac[...], preferred_element_type=F32), occ)
            leave(0, k)
        for g in range(1, len(outs)):
            for k in (1, 0, 2):
                leave(g, k)

    def own_rows():
        z_send[...] = pack(jnp.dot(w_v[rows_at(x * chunk, chunk, 256), :], ac[...], preferred_element_type=F32), occ)

    def col_terms():
        col_all[...] = pack(jnp.dot(wat[...], ar[...], preferred_element_type=F32), occ)
        out = []
        for m in reversed(range(len(team))):
            yy, cc = mates[m]
            part = rows_at(cc * packed + (yy ^ 1) * 2 * piece, 2 * piece)
            out.append(start(col_all.at[part], team_recv.at[m], gd_sems.at[0, m], gd_sems.at[1, m], team[m]))
        return out

    def col_out():
        for copy in gd:
            copy.wait_recv()
        total = col_all[rows_at(core * packed + pair * 2 * piece, 2 * piece), :]
        for m in range(len(team)):
            total = total + team_recv[m]
        col_send[...] = total
        for l in range(2):
            part = pl.ds(l * piece, piece)
            start(col_send.at[part], col_recv.at[zh], co_sems.at[0, l], co_sems.at[1, zh], writers[l])

    def all_in(copies):
        for copy in copies:
            copy.wait_recv()

    ga = share()
    all_in(xa)
    gd = col_terms()
    all_in(ga)
    row_terms()
    own_rows()
    col_out()

    ze = []
    for g, (first, count, waits) in enumerate(outs):
        all_in(xd[g])
        part = rows_at(first * piece, count * piece)
        total = z_send[part, :]
        for k in range(XN - 1):
            total = total + x_recv[k, part, :]
        z_send[part, :] = total
        for k in reversed(waits):
            where = rows_at((zl ^ (k + 1)) * piece, piece)
            ze.append(start(z_send.at[where], z_recv.at[k], ze_sems.at[0, k], ze_sems.at[1, k], z_peers[k]))

    result = z_send[rows_at(zl * piece, piece), :]
    all_in(ze)
    for k in range(ZN - 1):
        result = result + z_recv[k]
    for h in range(HN):
        remote(col_send.at[pl.ds(0, piece)], col_recv.at[h], co_sems.at[0, 0], co_sems.at[1, h], readers[h]).wait_recv()
    for h in range(HN):
        result = result + col_recv[h]
    out_ref[...] = unpack(result, occ)[:, :occ]

    for copy in sent:
        copy.wait_send()


def local(amplitudes, integrals, owner):
    occ, shard = amplitudes.shape
    rows, cols = integrals.shape
    packed = rows // XN * 3 // 4
    piece = packed // ZN
    dma = pltpu.SemaphoreType.DMA
    hbm = pl.BlockSpec(memory_space=pltpu.HBM)
    turned = pl.pallas_call(
        kernel,
        out_shape=jax.ShapeDtypeStruct((shard, occ), F32),
        in_specs=[hbm, hbm, hbm],
        out_specs=pl.BlockSpec(memory_space=pltpu.VMEM),
        scratch_shapes=[
            pltpu.VMEM((shard, occ), BF16),
            pltpu.VMEM((rows, cols), BF16),
            pltpu.VMEM((cols, rows), BF16),
            pltpu.SMEM((rows // TB, owner.shape[1]), jnp.int32),
            pltpu.VMEM((rows, LANES), BF16),
            pltpu.VMEM((cols, LANES), BF16),
            pltpu.VMEM((XN - 1, packed, LANES), F32),
            pltpu.VMEM((XN - 1, packed, LANES), F32),
            pltpu.VMEM((2 * packed, LANES), F32),
            pltpu.VMEM((2 * YN - 1, 2 * piece, LANES), F32),
            pltpu.VMEM((2 * piece, LANES), F32),
            pltpu.VMEM((HN, piece, LANES), F32),
            pltpu.VMEM((packed, LANES), F32),
            pltpu.VMEM((ZN - 1, piece, LANES), F32),
            dma((3,)),
            dma((2, ZN - 1)),
            dma((2, 3, XN - 1)),
            dma((2, 2)),
            dma((2, 2 * YN - 1)),
            dma((2, 2 * YN - 1)),
            dma((2, 2)),
            dma((2, 3, XN - 1)),
            dma((2, ZN - 1)),
        ],
        compiler_params=pltpu.CompilerParams(
            collective_id=0, has_side_effects=True, vmem_limit_bytes=56 * 1024 * 1024
        ),
    )(amplitudes.T, integrals, owner)
    return turned.T


def solution(mesh):
    in_specs = (P(None, ("row", "col")), P("row", "col"), P())
    out_specs = P(None, ("row", "col"))
    return jax.shard_map(local, mesh=mesh, in_specs=in_specs, out_specs=out_specs, check_vma=False)
```

```python
import jax
import jax.numpy as jnp
from jax import lax
from jax.experimental import pallas as pl
from jax.experimental.pallas import tpu as pltpu
from jax.sharding import PartitionSpec as P

TB = 128
LANES = 128
XN, YN, ZN, HN = 4, 4, 8, 2
MESH = pl.DeviceIdType.MESH
F32 = jnp.float32
BF16 = jnp.bfloat16


def pack(block, occ):
    lane = lax.broadcasted_iota(jnp.int32, (8, LANES), 1)
    out = []
    for s in range(block.shape[0] // 32):
        last = block[s * 32 + 24 : s * 32 + 32]
        for j in range(3):
            moved = pltpu.roll(last, occ - 32 * j, 1)
            out.append(jnp.where(lane < occ, block[s * 32 + 8 * j : s * 32 + 8 * j + 8], moved))
    return jnp.concatenate(out, axis=0)


def unpack(block, occ):
    lane = lax.broadcasted_iota(jnp.int32, (8, LANES), 1)
    last = jnp.zeros((8, LANES), F32)
    for j in range(3):
        moved = pltpu.roll(block[8 * j : 8 * j + 8], (LANES - occ + 32 * j) % LANES, 1)
        last = jnp.where((lane >= 32 * j) & (lane < 32 * j + 32), moved, last)
    return jnp.concatenate([block, last], axis=0)


def kernel(
    amp_hbm, w_hbm, owner_hbm, out_ref,
    amp_v, w_v, wat, own_s, ar, ac, row_send, x_recv, col_all, team_recv, col_send, col_recv, z_send, z_recv,
    copy_sems, za_sems, xa_sems, ci_sems, ga_sems, gd_sems, co_sems, xd_sems, ze_sems, ready,
):
    shard, occ = amp_v.shape
    rows, cols = w_v.shape
    row_tiles, col_tiles = rows // TB, cols // TB
    chunk = rows // XN
    packed = chunk * 3 // 4
    piece = packed // ZN
    r = lax.axis_index("row")
    c = lax.axis_index("col")
    y, zh, core = r // 4, (r // 2) % 2, r % 2
    x, zl = c // 8, c % 8

    def at(yy, zz, cc, xx, ll):
        return (yy * 4 + zz * 2 + cc, xx * 8 + ll)

    def rows_at(start, size, unit=8):
        return pl.ds(pl.multiple_of(start, unit), size)

    z_peers = [at(y, zh, core, x, zl ^ k) for k in range(1, ZN)]
    x_peers = [at(y, zh, core, x ^ k, zl) for k in range(1, XN)]
    mates = [(y ^ (m // 2), core ^ (m % 2)) for m in range(1, 2 * YN)]
    team = [at(yy, zh, cc, x, zl) for yy, cc in mates]

    def pair_of(yy):
        return (zl // 2) ^ ((yy - x) % 4) ^ jnp.where(zh == zl // 4, 3, 0)

    pair = pair_of(y)

    def reader(hh):
        line = 4 * zh + 2 * core + x // 2
        turn = (zl // 2) ^ (line // 2) ^ jnp.where(zh == hh, 3, 0)
        return at((y + turn) % 4, hh, x % 2, y, line)

    readers = [reader(hh) for hh in range(HN)]
    writers = [at(x, zl // 4, (zl // 2) % 2, 2 * (zl % 2) + core, 2 * pair + l) for l in range(2)]

    barrier = pltpu.get_barrier_semaphore()
    ahead = zh == 0
    answering = (zh == 1) & (zl // 4 == 0)

    def greet(peers):
        for peer in peers:
            pl.semaphore_signal(barrier, inc=1, device_id=peer, device_id_type=MESH)

    pl.when(jnp.logical_not(answering))(lambda: greet(writers))
    pl.when(ahead)(lambda: greet(readers[1:]))
    always = z_peers[::-1] + team[::-1] + x_peers
    greet(always)

    amp_copy = pltpu.make_async_copy(amp_hbm, amp_v, copy_sems.at[0])
    amp_copy.start()
    own_copy = pltpu.make_async_copy(owner_hbm.at[rows_at(r * row_tiles, row_tiles)], own_s, copy_sems.at[1])
    own_copy.start()
    w_copy = pltpu.make_async_copy(w_hbm, w_v, copy_sems.at[2])
    w_copy.start()

    amp_copy.wait()
    mine = rows_at(x * chunk + zl * shard, shard, 32)
    ar[mine, :] = jnp.concatenate([amp_v[...], jnp.zeros((shard, LANES - occ), BF16)], axis=1)
    pl.semaphore_wait(barrier, len(always) + HN - ahead.astype(jnp.int32) + 2 * answering.astype(jnp.int32))

    @pl.when(answering)
    def _():
        for peer in writers:
            pl.semaphore_signal(ready, inc=1, device_id=peer, device_id_type=MESH)

    def remote(src, dst, send_sem, recv_sem, peer):
        return pltpu.make_async_remote_copy(
            src_ref=src, dst_ref=dst, send_sem=send_sem, recv_sem=recv_sem, device_id=peer, device_id_type=MESH
        )

    sent = []

    def start(*args):
        copy = remote(*args)
        copy.start()
        sent.append(copy)
        return copy

    za = [None] * (ZN - 1)
    slot = rows_at((x % 2) * chunk + zl * shard, shard, 32)

    def to_line():
        for k in reversed(range(ZN - 1)):
            za[k] = start(ar.at[mine], ar.at[mine], za_sems.at[0, k], za_sems.at[1, k], z_peers[k])

    ci = [
        remote(ar.at[mine], ac.at[slot], ci_sems.at[0, k], ci_sems.at[1, zl % 2], readers[k]) for k in range(HN)
    ]
    sent += ci
    ci[0].start()
    pl.when(jnp.logical_not(ahead))(ci[1].start)
    to_line()

    w_copy.wait()
    own_copy.wait()
    for i in range(row_tiles):
        for j in range(col_tiles):
            held = own_s[i, c * col_tiles + j] == 1
            tile = w_v[i * TB : (i + 1) * TB, j * TB : (j + 1) * TB]
            kept = jnp.where(held, tile, jnp.zeros_like(tile))
            w_v[i * TB : (i + 1) * TB, j * TB : (j + 1) * TB] = kept
            away = jnp.where(r * row_tiles + i == c * col_tiles + j, jnp.zeros_like(tile), kept)
            wat[j * TB : (j + 1) * TB, i * TB : (i + 1) * TB] = away.T

    groups = [(zl // 4 * 4, 4, (0, 1, 2)), ((zl ^ 4) // 2 * 2, 2, (3, 4)), ((zl ^ 6) // 2 * 2, 2, (5, 6))]
    xa = []
    for g, (first, count, waits) in enumerate(groups):
        for k in waits:
            za[k].wait_recv()
        part = rows_at(x * chunk + first * shard, count * shard, 32)
        for k in (1, 0, 2):
            xa.append(start(ar.at[part], ar.at[part], xa_sems.at[0, g, k], xa_sems.at[1, g, k], x_peers[k]))

    fetched = rows_at(core * chunk + pair * 2 * shard, 2 * shard, 64)

    def answer():
        pl.semaphore_wait(ready, 1)
        ci[1].start()

    ga = [remote(ac.at[fetched], ac.at[fetched], ga_sems.at[0, m], ga_sems.at[1, m], team[m]) for m in range(len(team))]
    sent += ga

    def share():
        for l in range(2):
            remote(ar.at[mine], ac.at[slot], ci_sems.at[0, 0], ci_sems.at[1, l], writers[l]).wait_recv()
        for copy in reversed(ga):
            copy.start()

    outs = list(reversed(groups))
    xd = [[None] * (XN - 1) for _ in outs]

    def leave(g, k):
        first, count, _ = outs[g]
        part = rows_at(first * piece, count * piece)
        xd[g][k] = start(
            row_send.at[k, part], x_recv.at[k, part], xd_sems.at[0, g, k], xd_sems.at[1, g, k], x_peers[k]
        )

    def row_terms():
        for k in (1, 0, 2):
            theirs = rows_at((x ^ (k + 1)) * chunk, chunk, 256)
            row_send[k] = pack(jnp.dot(w_v[theirs, :], ac[...], preferred_element_type=F32), occ)
            leave(0, k)
        for g in range(1, len(outs)):
            for k in (1, 0, 2):
                leave(g, k)

    def own_rows():
        z_send[...] = pack(jnp.dot(w_v[rows_at(x * chunk, chunk, 256), :], ac[...], preferred_element_type=F32), occ)

    def col_terms():
        col_all[...] = pack(jnp.dot(wat[...], ar[...], preferred_element_type=F32), occ)
        out = []
        for m in reversed(range(len(team))):
            yy, cc = mates[m]
            part = rows_at(cc * packed + pair_of(yy) * 2 * piece, 2 * piece)
            out.append(start(col_all.at[part], team_recv.at[m], gd_sems.at[0, m], gd_sems.at[1, m], team[m]))
        return out

    def col_out():
        for copy in gd:
            copy.wait_recv()
        total = col_all[rows_at(core * packed + pair * 2 * piece, 2 * piece), :]
        for m in range(len(team)):
            total = total + team_recv[m]
        col_send[...] = total
        for copy in co:
            copy.start()

    co = [
        remote(
            col_send.at[pl.ds(l * piece, piece)], col_recv.at[zh], co_sems.at[0, l], co_sems.at[1, zh], writers[l]
        )
        for l in range(2)
    ]
    sent += co

    def all_in(copies):
        for copy in copies:
            copy.wait_recv()

    behind = jnp.logical_not(ahead)
    pl.when(ahead)(answer)
    pl.when(ahead)(share)
    all_in(xa)
    gd = col_terms()
    pl.when(behind)(col_out)
    pl.when(behind)(share)
    all_in(ga)
    row_terms()
    pl.when(ahead)(col_out)
    own_rows()

    ze = []
    for g, (first, count, waits) in enumerate(outs):
        all_in(xd[g])
        part = rows_at(first * piece, count * piece)
        total = z_send[part, :]
        for k in range(XN - 1):
            total = total + x_recv[k, part, :]
        z_send[part, :] = total
        for k in reversed(waits):
            where = rows_at((zl ^ (k + 1)) * piece, piece)
            ze.append(start(z_send.at[where], z_recv.at[k], ze_sems.at[0, k], ze_sems.at[1, k], z_peers[k]))

    result = z_send[rows_at(zl * piece, piece), :]
    all_in(ze)
    for k in range(ZN - 1):
        result = result + z_recv[k]
    for h in range(HN):
        remote(col_send.at[pl.ds(0, piece)], col_recv.at[h], co_sems.at[0, 0], co_sems.at[1, h], readers[h]).wait_recv()
    for h in range(HN):
        result = result + col_recv[h]
    out_ref[...] = unpack(result, occ)[:, :occ]

    for copy in sent:
        copy.wait_send()


def local(amplitudes, integrals, owner):
    occ, shard = amplitudes.shape
    rows, cols = integrals.shape
    packed = rows // XN * 3 // 4
    piece = packed // ZN
    dma = pltpu.SemaphoreType.DMA
    hbm = pl.BlockSpec(memory_space=pltpu.HBM)
    turned = pl.pallas_call(
        kernel,
        out_shape=jax.ShapeDtypeStruct((shard, occ), F32),
        in_specs=[hbm, hbm, hbm],
        out_specs=pl.BlockSpec(memory_space=pltpu.VMEM),
        scratch_shapes=[
            pltpu.VMEM((shard, occ), BF16),
            pltpu.VMEM((rows, cols), BF16),
            pltpu.VMEM((cols, rows), BF16),
            pltpu.SMEM((rows // TB, owner.shape[1]), jnp.int32),
            pltpu.VMEM((rows, LANES), BF16),
            pltpu.VMEM((cols, LANES), BF16),
            pltpu.VMEM((XN - 1, packed, LANES), F32),
            pltpu.VMEM((XN - 1, packed, LANES), F32),
            pltpu.VMEM((2 * packed, LANES), F32),
            pltpu.VMEM((2 * YN - 1, 2 * piece, LANES), F32),
            pltpu.VMEM((2 * piece, LANES), F32),
            pltpu.VMEM((HN, piece, LANES), F32),
            pltpu.VMEM((packed, LANES), F32),
            pltpu.VMEM((ZN - 1, piece, LANES), F32),
            dma((3,)),
            dma((2, ZN - 1)),
            dma((2, 3, XN - 1)),
            dma((2, 2)),
            dma((2, 2 * YN - 1)),
            dma((2, 2 * YN - 1)),
            dma((2, 2)),
            dma((2, 3, XN - 1)),
            dma((2, ZN - 1)),
            pltpu.SemaphoreType.REGULAR,
        ],
        compiler_params=pltpu.CompilerParams(
            collective_id=0, has_side_effects=True, vmem_limit_bytes=56 * 1024 * 1024
        ),
    )(amplitudes.T, integrals, owner)
    return turned.T


def solution(mesh):
    in_specs = (P(None, ("row", "col")), P("row", "col"), P())
    out_specs = P(None, ("row", "col"))
    return jax.shard_map(local, mesh=mesh, in_specs=in_specs, out_specs=out_specs, check_vma=False)
```

```python
import jax
import jax.numpy as jnp
from jax import lax
from jax.experimental import pallas as pl
from jax.experimental.pallas import tpu as pltpu
from jax.sharding import PartitionSpec as P

TB = 128
LANES = 128
XN, YN, ZN, HN = 4, 4, 8, 2
MESH = pl.DeviceIdType.MESH
F32 = jnp.float32
BF16 = jnp.bfloat16


def pack(block, occ):
    lane = lax.broadcasted_iota(jnp.int32, (8, LANES), 1)
    out = []
    for s in range(block.shape[0] // 32):
        last = block[s * 32 + 24 : s * 32 + 32]
        for j in range(3):
            moved = pltpu.roll(last, occ - 32 * j, 1)
            out.append(jnp.where(lane < occ, block[s * 32 + 8 * j : s * 32 + 8 * j + 8], moved))
    return jnp.concatenate(out, axis=0)


def unpack(block, occ):
    lane = lax.broadcasted_iota(jnp.int32, (8, LANES), 1)
    last = jnp.zeros((8, LANES), F32)
    for j in range(3):
        moved = pltpu.roll(block[8 * j : 8 * j + 8], (LANES - occ + 32 * j) % LANES, 1)
        last = jnp.where((lane >= 32 * j) & (lane < 32 * j + 32), moved, last)
    return jnp.concatenate([block, last], axis=0)


def kernel(
    amp_hbm, w_hbm, owner_hbm, out_ref,
    amp_v, w_v, wat, own_s, ar, ac, row_send, x_recv, col_all, team_recv, col_send, col_recv, z_send, z_recv,
    copy_sems, za_sems, xa_sems, ci_sems, ga_sems, gd_sems, co_sems, xd_sems, ze_sems, ready,
):
    shard, occ = amp_v.shape
    rows, cols = w_v.shape
    row_tiles, col_tiles = rows // TB, cols // TB
    chunk = rows // XN
    packed = chunk * 3 // 4
    piece = packed // ZN
    r = lax.axis_index("row")
    c = lax.axis_index("col")
    y, zh, core = r // 4, (r // 2) % 2, r % 2
    x, zl = c // 8, c % 8

    def at(yy, zz, cc, xx, ll):
        return (yy * 4 + zz * 2 + cc, xx * 8 + ll)

    def rows_at(start, size, unit=8):
        return pl.ds(pl.multiple_of(start, unit), size)

    z_peers = [at(y, zh, core, x, zl ^ k) for k in range(1, ZN)]
    x_peers = [at(y, zh, core, x ^ k, zl) for k in range(1, XN)]
    mates = [(y ^ (m // 2), core ^ (m % 2)) for m in range(1, 2 * YN)]
    team = [at(yy, zh, cc, x, zl) for yy, cc in mates]

    def pair_of(yy):
        return (zl // 2) ^ ((yy - x) % 4) ^ jnp.where(zh == zl // 4, 3, 0)

    pair = pair_of(y)

    def reader(hh):
        line = 4 * zh + 2 * core + x // 2
        turn = (zl // 2) ^ (line // 2) ^ jnp.where(zh == hh, 3, 0)
        return at((y + turn) % 4, hh, x % 2, y, line)

    readers = [reader(hh) for hh in range(HN)]
    writers = [at(x, zl // 4, (zl // 2) % 2, 2 * (zl % 2) + core, 2 * pair + l) for l in range(2)]

    barrier = pltpu.get_barrier_semaphore()
    ahead = zh == 0
    answering = (zh == 1) & (zl // 4 == 0)

    def greet(peers):
        for peer in peers:
            pl.semaphore_signal(barrier, inc=1, device_id=peer, device_id_type=MESH)

    pl.when(jnp.logical_not(answering))(lambda: greet(writers))
    pl.when(ahead)(lambda: greet(readers[1:]))
    always = z_peers[::-1] + team[::-1] + x_peers
    greet(always)

    amp_copy = pltpu.make_async_copy(amp_hbm, amp_v, copy_sems.at[0])
    amp_copy.start()
    own_copy = pltpu.make_async_copy(owner_hbm.at[rows_at(r * row_tiles, row_tiles)], own_s, copy_sems.at[1])
    own_copy.start()
    w_copy = pltpu.make_async_copy(w_hbm, w_v, copy_sems.at[2])
    w_copy.start()

    amp_copy.wait()
    mine = rows_at(x * chunk + zl * shard, shard, 32)
    ar[mine, :] = jnp.concatenate([amp_v[...], jnp.zeros((shard, LANES - occ), BF16)], axis=1)
    pl.semaphore_wait(barrier, len(always) + HN - ahead.astype(jnp.int32) + 2 * answering.astype(jnp.int32))

    @pl.when(answering)
    def _():
        for peer in writers:
            pl.semaphore_signal(ready, inc=1, device_id=peer, device_id_type=MESH)

    def remote(src, dst, send_sem, recv_sem, peer):
        return pltpu.make_async_remote_copy(
            src_ref=src, dst_ref=dst, send_sem=send_sem, recv_sem=recv_sem, device_id=peer, device_id_type=MESH
        )

    sent = []

    def start(*args):
        copy = remote(*args)
        copy.start()
        sent.append(copy)
        return copy

    za = [None] * (ZN - 1)
    slot = rows_at((x % 2) * chunk + zl * shard, shard, 32)

    def to_line():
        for k in reversed(range(ZN - 1)):
            za[k] = start(ar.at[mine], ar.at[mine], za_sems.at[0, k], za_sems.at[1, k], z_peers[k])

    ci = [
        remote(ar.at[mine], ac.at[slot], ci_sems.at[0, k], ci_sems.at[1, zl % 2], readers[k]) for k in range(HN)
    ]
    sent += ci
    ci[0].start()
    pl.when(jnp.logical_not(ahead))(ci[1].start)
    to_line()

    w_copy.wait()
    own_copy.wait()
    for i in range(row_tiles):
        for j in range(col_tiles):
            held = own_s[i, c * col_tiles + j] == 1
            tile = w_v[i * TB : (i + 1) * TB, j * TB : (j + 1) * TB]
            kept = jnp.where(held, tile, jnp.zeros_like(tile))
            w_v[i * TB : (i + 1) * TB, j * TB : (j + 1) * TB] = kept
            away = jnp.where(r * row_tiles + i == c * col_tiles + j, jnp.zeros_like(tile), kept)
            wat[j * TB : (j + 1) * TB, i * TB : (i + 1) * TB] = away.T

    groups = [(zl // 4 * 4, 4, (0, 1, 2)), ((zl ^ 4) // 2 * 2, 2, (3, 4)), ((zl ^ 6) // 2 * 2, 2, (5, 6))]
    xa = []
    for g, (first, count, waits) in enumerate(groups):
        for k in waits:
            za[k].wait_recv()
        part = rows_at(x * chunk + first * shard, count * shard, 32)
        for k in (1, 0, 2):
            xa.append(start(ar.at[part], ar.at[part], xa_sems.at[0, g, k], xa_sems.at[1, g, k], x_peers[k]))

    fetched = rows_at(core * chunk + pair * 2 * shard, 2 * shard, 64)

    def answer():
        pl.semaphore_wait(ready, 1)
        ci[1].start()

    ga = [remote(ac.at[fetched], ac.at[fetched], ga_sems.at[0, m], ga_sems.at[1, m], team[m]) for m in range(len(team))]
    sent += ga

    def share():
        for l in range(2):
            remote(ar.at[mine], ac.at[slot], ci_sems.at[0, 0], ci_sems.at[1, l], writers[l]).wait_recv()
        for copy in reversed(ga):
            copy.start()

    outs = list(reversed(groups))
    xd = [[None] * (XN - 1) for _ in outs]

    def leave(g, k):
        first, count, _ = outs[g]
        part = rows_at(first * piece, count * piece)
        xd[g][k] = start(
            row_send.at[k, part], x_recv.at[k, part], xd_sems.at[0, g, k], xd_sems.at[1, g, k], x_peers[k]
        )

    def row_terms():
        for k in (1, 0, 2):
            theirs = rows_at((x ^ (k + 1)) * chunk, chunk, 256)
            row_send[k] = pack(jnp.dot(w_v[theirs, :], ac[...], preferred_element_type=F32), occ)
            leave(0, k)
        for g in range(1, len(outs)):
            for k in (1, 0, 2):
                leave(g, k)

    def own_rows():
        z_send[...] = pack(jnp.dot(w_v[rows_at(x * chunk, chunk, 256), :], ac[...], preferred_element_type=F32), occ)

    def col_terms():
        col_all[...] = pack(jnp.dot(wat[...], ar[...], preferred_element_type=F32), occ)
        out = []
        for m in reversed(range(len(team))):
            yy, cc = mates[m]
            part = rows_at(cc * packed + pair_of(yy) * 2 * piece, 2 * piece)
            out.append(start(col_all.at[part], team_recv.at[m], gd_sems.at[0, m], gd_sems.at[1, m], team[m]))
        return out

    def col_out():
        for copy in gd:
            copy.wait_recv()
        total = col_all[rows_at(core * packed + pair * 2 * piece, 2 * piece), :]
        for m in range(len(team)):
            total = total + team_recv[m]
        col_send[...] = total
        for copy in co:
            copy.start()

    co = [
        remote(
            col_send.at[pl.ds(l * piece, piece)], col_recv.at[zh], co_sems.at[0, l], co_sems.at[1, zh], writers[l]
        )
        for l in range(2)
    ]
    sent += co

    def all_in(copies):
        for copy in copies:
            copy.wait_recv()

    behind = jnp.logical_not(ahead)
    pl.when(ahead)(answer)
    pl.when(ahead)(share)
    all_in(xa)
    gd = col_terms()
    pl.when(behind)(col_out)
    pl.when(behind)(share)
    all_in(ga)
    row_terms()
    pl.when(ahead)(col_out)
    own_rows()

    ze = []
    for g, (first, count, waits) in enumerate(outs):
        all_in(xd[g])
        part = rows_at(first * piece, count * piece)
        total = z_send[part, :]
        for k in range(XN - 1):
            total = total + x_recv[k, part, :]
        z_send[part, :] = total
        for k in reversed(waits):
            where = rows_at((zl ^ (k + 1)) * piece, piece)
            ze.append(start(z_send.at[where], z_recv.at[k], ze_sems.at[0, k], ze_sems.at[1, k], z_peers[k]))

    result = z_send[rows_at(zl * piece, piece), :]
    all_in(ze)
    for k in range(ZN - 1):
        result = result + z_recv[k]
    for h in range(HN):
        remote(col_send.at[pl.ds(0, piece)], col_recv.at[h], co_sems.at[0, 0], co_sems.at[1, h], readers[h]).wait_recv()
    for h in range(HN):
        result = result + col_recv[h]
    out_ref[...] = unpack(result, occ)[:, :occ]

    for copy in sent:
        copy.wait_send()


def local(amplitudes, integrals, owner):
    occ, shard = amplitudes.shape
    rows, cols = integrals.shape
    packed = rows // XN * 3 // 4
    piece = packed // ZN
    dma = pltpu.SemaphoreType.DMA
    hbm = pl.BlockSpec(memory_space=pltpu.HBM)
    turned = pl.pallas_call(
        kernel,
        out_shape=pltpu.VMEM((shard, occ), F32),
        in_specs=[hbm, hbm, hbm],
        out_specs=pl.BlockSpec(memory_space=pltpu.VMEM),
        scratch_shapes=[
            pltpu.VMEM((shard, occ), BF16),
            pltpu.VMEM((rows, cols), BF16),
            pltpu.VMEM((cols, rows), BF16),
            pltpu.SMEM((rows // TB, owner.shape[1]), jnp.int32),
            pltpu.VMEM((rows, LANES), BF16),
            pltpu.VMEM((cols, LANES), BF16),
            pltpu.VMEM((XN - 1, packed, LANES), F32),
            pltpu.VMEM((XN - 1, packed, LANES), F32),
            pltpu.VMEM((2 * packed, LANES), F32),
            pltpu.VMEM((2 * YN - 1, 2 * piece, LANES), F32),
            pltpu.VMEM((2 * piece, LANES), F32),
            pltpu.VMEM((HN, piece, LANES), F32),
            pltpu.VMEM((packed, LANES), F32),
            pltpu.VMEM((ZN - 1, piece, LANES), F32),
            dma((3,)),
            dma((2, ZN - 1)),
            dma((2, 3, XN - 1)),
            dma((2, 2)),
            dma((2, 2 * YN - 1)),
            dma((2, 2 * YN - 1)),
            dma((2, 2)),
            dma((2, 3, XN - 1)),
            dma((2, ZN - 1)),
            pltpu.SemaphoreType.REGULAR,
        ],
        compiler_params=pltpu.CompilerParams(
            collective_id=0, has_side_effects=True, vmem_limit_bytes=56 * 1024 * 1024
        ),
    )(amplitudes.T, integrals, owner)
    return turned.T


def solution(mesh):
    in_specs = (P(None, ("row", "col")), P("row", "col"), P())
    out_specs = P(None, ("row", "col"))
    return jax.shard_map(local, mesh=mesh, in_specs=in_specs, out_specs=out_specs, check_vma=False)
```

```python
import jax
import jax.numpy as jnp
from jax import lax
from jax.experimental import pallas as pl
from jax.experimental.pallas import tpu as pltpu
from jax.sharding import PartitionSpec as P

TB = 128
LANES = 128
XN, YN, ZN, HN = 4, 4, 8, 2
MESH = pl.DeviceIdType.MESH
F32 = jnp.float32
BF16 = jnp.bfloat16


def pack(block, occ):
    lane = lax.broadcasted_iota(jnp.int32, (8, LANES), 1)
    out = []
    for s in range(block.shape[0] // 32):
        last = block[s * 32 + 24 : s * 32 + 32]
        for j in range(3):
            moved = pltpu.roll(last, occ - 32 * j, 1)
            out.append(jnp.where(lane < occ, block[s * 32 + 8 * j : s * 32 + 8 * j + 8], moved))
    return jnp.concatenate(out, axis=0)


def unpack(block, occ):
    lane = lax.broadcasted_iota(jnp.int32, (8, LANES), 1)
    last = jnp.zeros((8, LANES), F32)
    for j in range(3):
        moved = pltpu.roll(block[8 * j : 8 * j + 8], (LANES - occ + 32 * j) % LANES, 1)
        last = jnp.where((lane >= 32 * j) & (lane < 32 * j + 32), moved, last)
    return jnp.concatenate([block, last], axis=0)


def kernel(
    amp_hbm, w_hbm, owner_hbm, out_ref,
    amp_v, w_v, wat, own_s, ar, ac, row_send, x_recv, col_all, team_recv, col_send, col_recv, z_send, z_recv,
    copy_sems, za_sems, xa_sems, ci_sems, ga_sems, gd_sems, co_sems, xd_sems, ze_sems, ready,
):
    shard, occ = amp_v.shape
    rows, cols = w_v.shape
    row_tiles, col_tiles = rows // TB, cols // TB
    chunk = rows // XN
    packed = chunk * 3 // 4
    piece = packed // ZN
    r = lax.axis_index("row")
    c = lax.axis_index("col")
    y, zh, core = r // 4, (r // 2) % 2, r % 2
    x, zl = c // 8, c % 8

    def at(yy, zz, cc, xx, ll):
        return (yy * 4 + zz * 2 + cc, xx * 8 + ll)

    def rows_at(start, size, unit=8):
        return pl.ds(pl.multiple_of(start, unit), size)

    z_peers = [at(y, zh, core, x, zl ^ k) for k in range(1, ZN)]
    x_peers = [at(y, zh, core, x ^ k, zl) for k in range(1, XN)]
    mates = [(y ^ (m // 2), core ^ (m % 2)) for m in range(1, 2 * YN)]
    team = [at(yy, zh, cc, x, zl) for yy, cc in mates]

    def pair_of(yy):
        return (zl // 2) ^ ((yy - x) % 4) ^ jnp.where(zh == zl // 4, 3, 0)

    pair = pair_of(y)

    def reader(hh):
        line = 4 * zh + 2 * core + x // 2
        turn = (zl // 2) ^ (line // 2) ^ jnp.where(zh == hh, 3, 0)
        return at((y + turn) % 4, hh, x % 2, y, line)

    readers = [reader(hh) for hh in range(HN)]
    writers = [at(x, zl // 4, (zl // 2) % 2, 2 * (zl % 2) + core, 2 * pair + l) for l in range(2)]

    barrier = pltpu.get_barrier_semaphore()
    ahead = zh == 0
    answering = (zh == 1) & (zl // 4 == 0)

    def greet(peers):
        for peer in peers:
            pl.semaphore_signal(barrier, inc=1, device_id=peer, device_id_type=MESH)

    pl.when(jnp.logical_not(answering))(lambda: greet(writers))
    pl.when(ahead)(lambda: greet(readers[1:]))
    always = z_peers[::-1] + team[::-1] + x_peers
    greet(always)

    amp_copy = pltpu.make_async_copy(amp_hbm, amp_v, copy_sems.at[0])
    amp_copy.start()
    own_copy = pltpu.make_async_copy(owner_hbm.at[rows_at(r * row_tiles, row_tiles)], own_s, copy_sems.at[1])
    own_copy.start()
    w_copy = pltpu.make_async_copy(w_hbm, w_v, copy_sems.at[2])
    w_copy.start()

    amp_copy.wait()
    mine = rows_at(x * chunk + zl * shard, shard, 32)
    ar[mine, :] = jnp.concatenate([amp_v[...], jnp.zeros((shard, LANES - occ), BF16)], axis=1)
    pl.semaphore_wait(barrier, len(always) + HN - ahead.astype(jnp.int32) + 2 * answering.astype(jnp.int32))

    @pl.when(answering)
    def _():
        for peer in writers:
            pl.semaphore_signal(ready, inc=1, device_id=peer, device_id_type=MESH)

    def remote(src, dst, send_sem, recv_sem, peer):
        return pltpu.make_async_remote_copy(
            src_ref=src, dst_ref=dst, send_sem=send_sem, recv_sem=recv_sem, device_id=peer, device_id_type=MESH
        )

    sent = []

    def start(*args):
        copy = remote(*args)
        copy.start()
        sent.append(copy)
        return copy

    za = [None] * (ZN - 1)
    slot = rows_at((x % 2) * chunk + zl * shard, shard, 32)

    def to_line():
        for k in reversed(range(ZN - 1)):
            za[k] = start(ar.at[mine], ar.at[mine], za_sems.at[0, k], za_sems.at[1, k], z_peers[k])

    ci = [
        remote(ar.at[mine], ac.at[slot], ci_sems.at[0, k], ci_sems.at[1, zl % 2], readers[k]) for k in range(HN)
    ]
    sent += ci
    ci[0].start()
    pl.when(jnp.logical_not(ahead))(ci[1].start)
    to_line()

    w_copy.wait()
    own_copy.wait()
    for i in range(row_tiles):
        for j in range(col_tiles):
            held = own_s[i, c * col_tiles + j] == 1
            tile = w_v[i * TB : (i + 1) * TB, j * TB : (j + 1) * TB]
            kept = jnp.where(held, tile, jnp.zeros_like(tile))
            w_v[i * TB : (i + 1) * TB, j * TB : (j + 1) * TB] = kept
            away = jnp.where(r * row_tiles + i == c * col_tiles + j, jnp.zeros_like(tile), kept)
            wat[j * TB : (j + 1) * TB, i * TB : (i + 1) * TB] = away.T

    groups = [(zl // 4 * 4, 4, (0, 1, 2)), ((zl ^ 4) // 2 * 2, 2, (3, 4)), ((zl ^ 6) // 2 * 2, 2, (5, 6))]
    xa = []
    for g, (first, count, waits) in enumerate(groups):
        for k in waits:
            za[k].wait_recv()
        part = rows_at(x * chunk + first * shard, count * shard, 32)
        for k in (1, 0, 2):
            xa.append(start(ar.at[part], ar.at[part], xa_sems.at[0, g, k], xa_sems.at[1, g, k], x_peers[k]))

    fetched = rows_at(core * chunk + pair * 2 * shard, 2 * shard, 64)

    def answer():
        pl.semaphore_wait(ready, 1)
        ci[1].start()

    ga = [remote(ac.at[fetched], ac.at[fetched], ga_sems.at[0, m], ga_sems.at[1, m], team[m]) for m in range(len(team))]
    sent += ga

    def share():
        for l in range(2):
            remote(ar.at[mine], ac.at[slot], ci_sems.at[0, 0], ci_sems.at[1, l], writers[l]).wait_recv()
        for copy in reversed(ga):
            copy.start()

    outs = [(zl ^ q, 1, (q - 1,)) for q in (7, 6, 5, 4)] + [groups[0]]
    xd = [[None] * (XN - 1) for _ in outs]

    def leave(g, k):
        first, count, _ = outs[g]
        part = rows_at(first * piece, count * piece)
        xd[g][k] = start(
            row_send.at[k, part], x_recv.at[k, part], xd_sems.at[0, g, k], xd_sems.at[1, g, k], x_peers[k]
        )

    def row_terms():
        for k in (1, 0, 2):
            theirs = rows_at((x ^ (k + 1)) * chunk, chunk, 256)
            row_send[k] = pack(jnp.dot(w_v[theirs, :], ac[...], preferred_element_type=F32), occ)
            leave(0, k)
        for g in range(1, len(outs)):
            for k in (1, 0, 2):
                leave(g, k)

    def own_rows():
        z_send[...] = pack(jnp.dot(w_v[rows_at(x * chunk, chunk, 256), :], ac[...], preferred_element_type=F32), occ)

    def col_terms():
        col_all[...] = pack(jnp.dot(wat[...], ar[...], preferred_element_type=F32), occ)
        out = []
        for m in reversed(range(len(team))):
            yy, cc = mates[m]
            part = rows_at(cc * packed + pair_of(yy) * 2 * piece, 2 * piece)
            out.append(start(col_all.at[part], team_recv.at[m], gd_sems.at[0, m], gd_sems.at[1, m], team[m]))
        return out

    def col_out():
        for copy in gd:
            copy.wait_recv()
        total = col_all[rows_at(core * packed + pair * 2 * piece, 2 * piece), :]
        for m in range(len(team)):
            total = total + team_recv[m]
        col_send[...] = total
        for copy in co:
            copy.start()

    co = [
        remote(
            col_send.at[pl.ds(l * piece, piece)], col_recv.at[zh], co_sems.at[0, l], co_sems.at[1, zh], writers[l]
        )
        for l in range(2)
    ]
    sent += co

    def all_in(copies):
        for copy in copies:
            copy.wait_recv()

    behind = jnp.logical_not(ahead)
    pl.when(ahead)(answer)
    pl.when(ahead)(share)
    all_in(xa)
    gd = col_terms()
    pl.when(behind)(col_out)
    pl.when(behind)(share)
    all_in(ga)
    row_terms()
    pl.when(ahead)(col_out)
    own_rows()

    ze = []
    for g, (first, count, waits) in enumerate(outs):
        all_in(xd[g])
        part = rows_at(first * piece, count * piece)
        total = z_send[part, :]
        for k in range(XN - 1):
            total = total + x_recv[k, part, :]
        z_send[part, :] = total
        for k in reversed(waits):
            where = rows_at((zl ^ (k + 1)) * piece, piece)
            ze.append(start(z_send.at[where], z_recv.at[k], ze_sems.at[0, k], ze_sems.at[1, k], z_peers[k]))

    result = z_send[rows_at(zl * piece, piece), :]
    all_in(ze)
    for k in range(ZN - 1):
        result = result + z_recv[k]
    for h in range(HN):
        remote(col_send.at[pl.ds(0, piece)], col_recv.at[h], co_sems.at[0, 0], co_sems.at[1, h], readers[h]).wait_recv()
    for h in range(HN):
        result = result + col_recv[h]
    out_ref[...] = unpack(result, occ)[:, :occ]

    for copy in sent:
        copy.wait_send()


def local(amplitudes, integrals, owner):
    occ, shard = amplitudes.shape
    rows, cols = integrals.shape
    packed = rows // XN * 3 // 4
    piece = packed // ZN
    dma = pltpu.SemaphoreType.DMA
    hbm = pl.BlockSpec(memory_space=pltpu.HBM)
    turned = pl.pallas_call(
        kernel,
        out_shape=pltpu.VMEM((shard, occ), F32),
        in_specs=[hbm, hbm, hbm],
        out_specs=pl.BlockSpec(memory_space=pltpu.VMEM),
        scratch_shapes=[
            pltpu.VMEM((shard, occ), BF16),
            pltpu.VMEM((rows, cols), BF16),
            pltpu.VMEM((cols, rows), BF16),
            pltpu.SMEM((rows // TB, owner.shape[1]), jnp.int32),
            pltpu.VMEM((rows, LANES), BF16),
            pltpu.VMEM((cols, LANES), BF16),
            pltpu.VMEM((XN - 1, packed, LANES), F32),
            pltpu.VMEM((XN - 1, packed, LANES), F32),
            pltpu.VMEM((2 * packed, LANES), F32),
            pltpu.VMEM((2 * YN - 1, 2 * piece, LANES), F32),
            pltpu.VMEM((2 * piece, LANES), F32),
            pltpu.VMEM((HN, piece, LANES), F32),
            pltpu.VMEM((packed, LANES), F32),
            pltpu.VMEM((ZN - 1, piece, LANES), F32),
            dma((3,)),
            dma((2, ZN - 1)),
            dma((2, 3, XN - 1)),
            dma((2, 2)),
            dma((2, 2 * YN - 1)),
            dma((2, 2 * YN - 1)),
            dma((2, 2)),
            dma((2, 5, XN - 1)),
            dma((2, ZN - 1)),
            pltpu.SemaphoreType.REGULAR,
        ],
        compiler_params=pltpu.CompilerParams(
            collective_id=0, has_side_effects=True, vmem_limit_bytes=56 * 1024 * 1024
        ),
    )(amplitudes.T, integrals, owner)
    return turned.T


def solution(mesh):
    in_specs = (P(None, ("row", "col")), P("row", "col"), P())
    out_specs = P(None, ("row", "col"))
    return jax.shard_map(local, mesh=mesh, in_specs=in_specs, out_specs=out_specs, check_vma=False)
```

```python
import jax
import jax.numpy as jnp
from jax import lax
from jax.experimental import pallas as pl
from jax.experimental.pallas import tpu as pltpu
from jax.sharding import PartitionSpec as P

TB = 128
LANES = 128
XN, YN, ZN, HN = 4, 4, 8, 2
MESH = pl.DeviceIdType.MESH
F32 = jnp.float32
BF16 = jnp.bfloat16


def pack(block, occ):
    lane = lax.broadcasted_iota(jnp.int32, (8, LANES), 1)
    out = []
    for s in range(block.shape[0] // 32):
        last = block[s * 32 + 24 : s * 32 + 32]
        for j in range(3):
            moved = pltpu.roll(last, occ - 32 * j, 1)
            out.append(jnp.where(lane < occ, block[s * 32 + 8 * j : s * 32 + 8 * j + 8], moved))
    return jnp.concatenate(out, axis=0)


def unpack(block, occ):
    lane = lax.broadcasted_iota(jnp.int32, (8, LANES), 1)
    last = jnp.zeros((8, LANES), F32)
    for j in range(3):
        moved = pltpu.roll(block[8 * j : 8 * j + 8], (LANES - occ + 32 * j) % LANES, 1)
        last = jnp.where((lane >= 32 * j) & (lane < 32 * j + 32), moved, last)
    return jnp.concatenate([block, last], axis=0)


def kernel(
    amp_hbm, w_hbm, owner_hbm, out_ref,
    amp_v, w_v, wat, own_s, ar, ac, row_send, x_recv, col_all, team_recv, col_send, col_recv, z_send, z_recv,
    copy_sems, za_sems, xa_sems, ci_sems, ga_sems, gd_sems, co_sems, xd_sems, ze_sems, ready,
):
    shard, occ = amp_v.shape
    rows, cols = w_v.shape
    row_tiles, col_tiles = rows // TB, cols // TB
    chunk = rows // XN
    packed = chunk * 3 // 4
    piece = packed // ZN
    r = lax.axis_index("row")
    c = lax.axis_index("col")
    y, zh, core = r // 4, (r // 2) % 2, r % 2
    x, zl = c // 8, c % 8

    def at(yy, zz, cc, xx, ll):
        return (yy * 4 + zz * 2 + cc, xx * 8 + ll)

    def rows_at(start, size, unit=8):
        return pl.ds(pl.multiple_of(start, unit), size)

    z_peers = [at(y, zh, core, x, zl ^ k) for k in range(1, ZN)]
    x_peers = [at(y, zh, core, x ^ k, zl) for k in range(1, XN)]
    mates = [(y ^ (m // 2), core ^ (m % 2)) for m in range(1, 2 * YN)]
    team = [at(yy, zh, cc, x, zl) for yy, cc in mates]

    def pair_of(yy):
        return (zl // 2) ^ ((yy - x) % 4) ^ jnp.where(zh == zl // 4, 3, 0)

    pair = pair_of(y)

    def reader(hh):
        line = 4 * zh + 2 * core + x // 2
        turn = (zl // 2) ^ (line // 2) ^ jnp.where(zh == hh, 3, 0)
        return at((y + turn) % 4, hh, x % 2, y, line)

    readers = [reader(hh) for hh in range(HN)]
    writers = [at(x, zl // 4, (zl // 2) % 2, 2 * (zl % 2) + core, 2 * pair + l) for l in range(2)]

    amp_copy = pltpu.make_async_copy(amp_hbm, amp_v, copy_sems.at[0])
    amp_copy.start()
    own_copy = pltpu.make_async_copy(owner_hbm.at[rows_at(r * row_tiles, row_tiles)], own_s, copy_sems.at[1])
    own_copy.start()
    w_copy = pltpu.make_async_copy(w_hbm, w_v, copy_sems.at[2])
    w_copy.start()

    barrier = pltpu.get_barrier_semaphore()
    ahead = zh == 0
    answering = (zh == 1) & (zl // 4 == 0)

    def greet(peers):
        for peer in peers:
            pl.semaphore_signal(barrier, inc=1, device_id=peer, device_id_type=MESH)

    pl.when(jnp.logical_not(answering))(lambda: greet(writers))
    pl.when(ahead)(lambda: greet(readers[1:]))
    always = z_peers[::-1] + team[::-1] + x_peers
    greet(always)

    amp_copy.wait()
    mine = rows_at(x * chunk + zl * shard, shard, 32)
    ar[mine, :] = jnp.concatenate([amp_v[...], jnp.zeros((shard, LANES - occ), BF16)], axis=1)
    pl.semaphore_wait(barrier, len(always) + HN - ahead.astype(jnp.int32) + 2 * answering.astype(jnp.int32))

    @pl.when(answering)
    def _():
        for peer in writers:
            pl.semaphore_signal(ready, inc=1, device_id=peer, device_id_type=MESH)

    def remote(src, dst, send_sem, recv_sem, peer):
        return pltpu.make_async_remote_copy(
            src_ref=src, dst_ref=dst, send_sem=send_sem, recv_sem=recv_sem, device_id=peer, device_id_type=MESH
        )

    sent = []

    def start(*args):
        copy = remote(*args)
        copy.start()
        sent.append(copy)
        return copy

    za = [None] * (ZN - 1)
    slot = rows_at((x % 2) * chunk + zl * shard, shard, 32)

    def to_line():
        for k in reversed(range(ZN - 1)):
            za[k] = start(ar.at[mine], ar.at[mine], za_sems.at[0, k], za_sems.at[1, k], z_peers[k])

    ci = [
        remote(ar.at[mine], ac.at[slot], ci_sems.at[0, k], ci_sems.at[1, zl % 2], readers[k]) for k in range(HN)
    ]
    sent += ci
    ci[0].start()
    pl.when(jnp.logical_not(ahead))(ci[1].start)
    to_line()

    w_copy.wait()
    own_copy.wait()
    for i in range(row_tiles):
        for j in range(col_tiles):
            held = own_s[i, c * col_tiles + j] == 1
            tile = w_v[i * TB : (i + 1) * TB, j * TB : (j + 1) * TB]
            kept = jnp.where(held, tile, jnp.zeros_like(tile))
            w_v[i * TB : (i + 1) * TB, j * TB : (j + 1) * TB] = kept
            away = jnp.where(r * row_tiles + i == c * col_tiles + j, jnp.zeros_like(tile), kept)
            wat[j * TB : (j + 1) * TB, i * TB : (i + 1) * TB] = away.T

    groups = [(zl // 4 * 4, 4, (0, 1, 2)), ((zl ^ 4) // 2 * 2, 2, (3, 4)), ((zl ^ 6) // 2 * 2, 2, (5, 6))]
    xa = []
    for g, (first, count, waits) in enumerate(groups):
        for k in waits:
            za[k].wait_recv()
        part = rows_at(x * chunk + first * shard, count * shard, 32)
        for k in (1, 0, 2):
            xa.append(start(ar.at[part], ar.at[part], xa_sems.at[0, g, k], xa_sems.at[1, g, k], x_peers[k]))

    fetched = rows_at(core * chunk + pair * 2 * shard, 2 * shard, 64)

    def answer():
        pl.semaphore_wait(ready, 1)
        ci[1].start()

    ga = [remote(ac.at[fetched], ac.at[fetched], ga_sems.at[0, m], ga_sems.at[1, m], team[m]) for m in range(len(team))]
    sent += ga

    def share():
        for l in range(2):
            remote(ar.at[mine], ac.at[slot], ci_sems.at[0, 0], ci_sems.at[1, l], writers[l]).wait_recv()
        for copy in (ga[m] for m in (4, 3, 6, 5, 2, 1, 0)):
            copy.start()

    outs = [(zl ^ q, 1, (q - 1,)) for q in (7, 6, 5, 4)] + [groups[0]]
    xd = [[None] * (XN - 1) for _ in outs]

    def leave(g, k):
        first, count, _ = outs[g]
        part = rows_at(first * piece, count * piece)
        xd[g][k] = start(
            row_send.at[k, part], x_recv.at[k, part], xd_sems.at[0, g, k], xd_sems.at[1, g, k], x_peers[k]
        )

    def row_terms():
        for k in (1, 0, 2):
            theirs = rows_at((x ^ (k + 1)) * chunk, chunk, 256)
            row_send[k] = pack(jnp.dot(w_v[theirs, :], ac[...], preferred_element_type=F32), occ)
            leave(0, k)
        for g in range(1, len(outs)):
            for k in (1, 0, 2):
                leave(g, k)

    def own_rows():
        z_send[...] = pack(jnp.dot(w_v[rows_at(x * chunk, chunk, 256), :], ac[...], preferred_element_type=F32), occ)

    def col_terms():
        col_all[...] = pack(jnp.dot(wat[...], ar[...], preferred_element_type=F32), occ)
        out = []
        for m in (4, 3, 6, 5, 2, 1, 0):
            yy, cc = mates[m]
            part = rows_at(cc * packed + pair_of(yy) * 2 * piece, 2 * piece)
            out.append(start(col_all.at[part], team_recv.at[m], gd_sems.at[0, m], gd_sems.at[1, m], team[m]))
        return out

    def col_out():
        for copy in gd:
            copy.wait_recv()
        total = col_all[rows_at(core * packed + pair * 2 * piece, 2 * piece), :]
        for m in range(len(team)):
            total = total + team_recv[m]
        col_send[...] = total
        for copy in co:
            copy.start()

    co = [
        remote(
            col_send.at[pl.ds(l * piece, piece)], col_recv.at[zh], co_sems.at[0, l], co_sems.at[1, zh], writers[l]
        )
        for l in range(2)
    ]
    sent += co

    def all_in(copies):
        for copy in copies:
            copy.wait_recv()

    behind = jnp.logical_not(ahead)
    pl.when(ahead)(answer)
    pl.when(ahead)(share)
    all_in(xa)
    gd = col_terms()
    pl.when(behind)(col_out)
    pl.when(behind)(share)
    all_in(ga)
    row_terms()
    pl.when(ahead)(col_out)
    own_rows()

    ze = []
    for g, (first, count, waits) in enumerate(outs):
        all_in(xd[g])
        part = rows_at(first * piece, count * piece)
        total = z_send[part, :]
        for k in range(XN - 1):
            total = total + x_recv[k, part, :]
        z_send[part, :] = total
        for k in reversed(waits):
            where = rows_at((zl ^ (k + 1)) * piece, piece)
            ze.append(start(z_send.at[where], z_recv.at[k], ze_sems.at[0, k], ze_sems.at[1, k], z_peers[k]))

    result = z_send[rows_at(zl * piece, piece), :]
    all_in(ze)
    for k in range(ZN - 1):
        result = result + z_recv[k]
    for h in range(HN):
        remote(col_send.at[pl.ds(0, piece)], col_recv.at[h], co_sems.at[0, 0], co_sems.at[1, h], readers[h]).wait_recv()
    for h in range(HN):
        result = result + col_recv[h]
    out_ref[...] = unpack(result, occ)[:, :occ]

    for copy in sent:
        copy.wait_send()


def local(amplitudes, integrals, owner):
    occ, shard = amplitudes.shape
    rows, cols = integrals.shape
    packed = rows // XN * 3 // 4
    piece = packed // ZN
    dma = pltpu.SemaphoreType.DMA
    hbm = pl.BlockSpec(memory_space=pltpu.HBM)
    turned = pl.pallas_call(
        kernel,
        out_shape=pltpu.VMEM((shard, occ), F32),
        in_specs=[hbm, hbm, hbm],
        out_specs=pl.BlockSpec(memory_space=pltpu.VMEM),
        scratch_shapes=[
            pltpu.VMEM((shard, occ), BF16),
            pltpu.VMEM((rows, cols), BF16),
            pltpu.VMEM((cols, rows), BF16),
            pltpu.SMEM((rows // TB, owner.shape[1]), jnp.int32),
            pltpu.VMEM((rows, LANES), BF16),
            pltpu.VMEM((cols, LANES), BF16),
            pltpu.VMEM((XN - 1, packed, LANES), F32),
            pltpu.VMEM((XN - 1, packed, LANES), F32),
            pltpu.VMEM((2 * packed, LANES), F32),
            pltpu.VMEM((2 * YN - 1, 2 * piece, LANES), F32),
            pltpu.VMEM((2 * piece, LANES), F32),
            pltpu.VMEM((HN, piece, LANES), F32),
            pltpu.VMEM((packed, LANES), F32),
            pltpu.VMEM((ZN - 1, piece, LANES), F32),
            dma((3,)),
            dma((2, ZN - 1)),
            dma((2, 3, XN - 1)),
            dma((2, 2)),
            dma((2, 2 * YN - 1)),
            dma((2, 2 * YN - 1)),
            dma((2, 2)),
            dma((2, 5, XN - 1)),
            dma((2, ZN - 1)),
            pltpu.SemaphoreType.REGULAR,
        ],
        compiler_params=pltpu.CompilerParams(
            collective_id=0, has_side_effects=True, vmem_limit_bytes=56 * 1024 * 1024
        ),
    )(amplitudes.T, integrals, owner)
    return turned.T


def solution(mesh):
    in_specs = (P(None, ("row", "col")), P("row", "col"), P())
    out_specs = P(None, ("row", "col"))
    return jax.shard_map(local, mesh=mesh, in_specs=in_specs, out_specs=out_specs, check_vma=False)
```
